32 devices in a mesh: win: 4 (over y, x), row: 2 (over core), col: 4 (over z).
Axes of the slice: x: 2, y: 2, z: 4, core: 2. Of those that a mesh axis runs over, the one named last changes fastest.
Arguments:
- spectra: bfloat16 [2, 8, 6144, 768], P(None, None, ('row', 'col'), 'win'), may hold values from -6 to 6
- gain: float32 [6144], P(('row', 'col')), may hold values from 0.1 to 3
Outputs:
- cross: float32 [2, 8, 6144, 6144], P(None, 'win', 'row', 'col')
The draws below stay inside these ranges and needn't reach their ends.
All inputs are finite; a program needn't handle non-finite values.
Results may differ from the reference program's by a relative error of at most 0.0038.
Values may be sent and summed in bfloat16 or wider, within the bound.
A program may use at most 256 MiB of HBM per device.

```python
import math
import jax
import jax.numpy as jnp
from jax import lax

C = 6144
F = 8
W = 768


def level_of(own_key, shape, pieces, least, top_value):
    level, own = 1.0, jax.random.fold_in(own_key, 6)
    for position, parts in pieces:
        draws = jnp.exp(jax.random.uniform(jax.random.fold_in(own, position), (parts,), jnp.float32, least / len(pieces), top_value / len(pieces)))
        level = level * jnp.repeat(draws, shape[position] // parts).reshape([-1 if axis == position else 1 for axis in range(len(shape))])
    return level


def scatter_about(key, extent, scale, reach, cuts=(), held_as=jnp.bfloat16):
    values = scale * jax.random.normal(key, extent, jnp.float32)
    if cuts:
        values = values * level_of(key, extent, cuts, -0.22, 0.18)
    return jnp.clip(values, -reach, reach).astype(held_as)


def setup_inputs(seed: int = 0) -> dict:
    key_of = jax.random.split(jax.random.key(seed), 3)
    return {
        "spectra": scatter_about(key_of[0], (2, F, C, W), 1.0, 6.0, ((2, 8), (3, 4))),
        "gain": jnp.clip(jnp.exp(math.log(3.0) - 3.4011974 * jax.random.uniform(key_of[1], (C,), jnp.float32) ** level_of(key_of[1], (C,), ((0, 8),), -0.2, 0.2)), 0.1, 3.0),
    }


def whiten(spectra, gain):
    calibrated = spectra.astype(jnp.float32) * gain[None, None, :, None]
    level = jnp.sqrt(lax.optimization_barrier(jnp.mean(calibrated * calibrated, axis=(0, 1))))
    return (calibrated / jnp.maximum(level, 0.5)).astype(jnp.bfloat16)

def reference(spectra, gain):
    white = whiten(spectra, gain)
    windows = white.shape[3]
    left_side = jnp.concatenate([white[0], white[1]], axis=-1)
    right_real = left_side
    right_imag = jnp.concatenate([-white[1], white[0]], axis=-1)

    def one_bin(operands):
        first = operands[0].astype(jnp.float32)
        second = operands[1].astype(jnp.float32)
        third = operands[2].astype(jnp.float32)
        real_part = jnp.dot(first, second.T, precision=lax.Precision.HIGHEST)
        imag_part = jnp.dot(first, third.T, precision=lax.Precision.HIGHEST)
        return jnp.stack([real_part, imag_part]) / jnp.float32(windows)
    stacked = lax.map(one_bin, (left_side, right_real, right_imag))
    return jnp.transpose(stacked, (1, 0, 2, 3))
```

```python
import functools

import jax
import jax.numpy as jnp
from jax import lax
from jax.experimental import pallas as pl
from jax.experimental.pallas import tpu as pltpu
from jax.sharding import PartitionSpec as P

MESH = pl.DeviceIdType.MESH


def broadcast(value, axis, source):
    kept = jnp.where(lax.axis_index(axis) == source, value, 0).astype(value.dtype)
    return lax.psum(kept, axis)


def per_device_collectives(spectra, gain):
    calibrated = spectra.astype(jnp.float32) * gain[None, None, :, None]
    level = jnp.sqrt(jnp.mean(calibrated * calibrated, axis=(0, 1)))
    white = (calibrated / jnp.maximum(level, 0.5)).astype(jnp.bfloat16)
    regrouped = lax.all_to_all(white, "win", split_axis=1, concat_axis=3, tiled=True)
    windows = regrouped.shape[3]
    rows_block = lax.all_gather(regrouped, "col", axis=2, tiled=True)
    ratio = lax.axis_size("col") // lax.axis_size("row")
    col_width = rows_block.shape[2] // ratio
    col_index = lax.axis_index("col")
    portion = col_index % ratio
    root_row = col_index // ratio
    relayed = broadcast(rows_block, "row", root_row)
    cols_block = lax.dynamic_slice_in_dim(relayed, portion * col_width, col_width, 2)
    left_side = jnp.concatenate([rows_block[0], rows_block[1]], axis=-1)
    right_real = jnp.concatenate([cols_block[0], cols_block[1]], axis=-1)
    right_imag = jnp.concatenate([-cols_block[1], cols_block[0]], axis=-1)
    right_both = jnp.stack([right_real, right_imag])
    stacked = jnp.einsum(
        "fiw,ofjw->ofij", left_side, right_both, preferred_element_type=jnp.float32
    )
    return stacked / jnp.float32(windows)


def whiten_kernel(x_ref, gain_ref, white_ref):
    parts, bins = x_ref.shape[:2]
    gain = gain_ref[...]
    total = jnp.zeros(x_ref.shape[2:], jnp.float32)
    for p in range(parts):
        for f in range(bins):
            calibrated = x_ref[p, f].astype(jnp.float32) * gain
            total += calibrated * calibrated
    level = jnp.sqrt(total * (1.0 / (parts * bins)))
    scale = 1.0 / jnp.maximum(level, 0.5)
    for p in range(parts):
        for f in range(bins):
            calibrated = x_ref[p, f].astype(jnp.float32) * gain
            white_ref[f, p] = (calibrated * scale).astype(white_ref.dtype)


def whiten(spectra, gain):
    parts, bins, channels, windows = spectra.shape
    tile = 32 if windows % 32 == 0 else 16
    return pl.pallas_call(
        whiten_kernel,
        grid=(windows // tile,),
        out_shape=jax.ShapeDtypeStruct((bins, parts, windows, channels), jnp.bfloat16),
        in_specs=[
            pl.BlockSpec((parts, bins, tile, channels), lambda i: (0, 0, i, 0)),
            pl.BlockSpec((1, channels), lambda i: (0, 0)),
        ],
        out_specs=pl.BlockSpec((bins, parts, tile, channels), lambda i: (0, 0, i, 0)),
        compiler_params=pltpu.CompilerParams(vmem_limit_bytes=32 * 2**20),
    )(jnp.swapaxes(spectra, 2, 3), gain[None])


class Gather:
    def __init__(self, sizes, white, rows, cols, sems):
        self.S, self.R, self.N = sizes
        self.white, self.rows, self.cols = white, rows, cols
        (self.own_sem, self.swap_send, self.swap_recv, self.down_send, self.down_recv, self.up_send, self.up_recv,
         self.col_own, self.col_send, self.col_recv) = sems
        self.w, self.r, self.c = lax.axis_index("win"), lax.axis_index("row"), lax.axis_index("col")
        self.bins = rows.shape[0]
        ratio = self.N // self.R
        self.first_col = (self.c % ratio) * self.R
        self.is_root = self.r == self.c // ratio
        self.col_reach = max(
            abs((c % ratio) * self.R + q - c) for c in range(self.N) for q in range(self.R)
        )

    def partner(self, d):
        half = self.S // 2
        return ((self.w // 2 + d // 2) % half) * 2 + (self.w + d) % 2

    def barrier(self):
        sem = pltpu.get_barrier_semaphore()
        for d in range(1, self.S):
            pl.semaphore_signal(sem, inc=1, device_id={"win": self.partner(d)}, device_id_type=MESH)
        for e in range(1, self.R):
            pl.semaphore_signal(sem, inc=1, device_id={"row": (self.r + e) % self.R}, device_id_type=MESH)

        @pl.when(self.c > 0)
        def _():
            pl.semaphore_signal(sem, inc=1, device_id={"col": self.c - 1}, device_id_type=MESH)

        @pl.when(self.c < self.N - 1)
        def _():
            pl.semaphore_signal(sem, inc=1, device_id={"col": self.c + 1}, device_id_type=MESH)

        ends = (self.c == 0).astype(jnp.int32) + (self.c == self.N - 1).astype(jnp.int32)
        pl.semaphore_wait(sem, self.S - 1 + self.R - 1 + 2 - ends)

    def keep(self, b):
        return pltpu.make_async_copy(self.white.at[self.w, b], self.rows.at[b, self.c, 0], self.own_sem.at[b])

    def swap(self, b, d):
        p = self.partner(d)
        return pltpu.make_async_remote_copy(
            src_ref=self.white.at[p, b], dst_ref=self.rows.at[b, self.c, d],
            send_sem=self.swap_send.at[b, d], recv_sem=self.swap_recv.at[b, d],
            device_id={"win": p}, device_id_type=MESH)

    def down(self, b, t, d):
        block = self.c + t
        src = self.white.at[self.w, b] if t == 0 and d == 0 else self.rows.at[b, block, d]
        return pltpu.make_async_remote_copy(
            src_ref=src, dst_ref=self.rows.at[b, block, d],
            send_sem=self.down_send.at[b, t, d], recv_sem=self.down_recv.at[b, t, d],
            device_id={"col": self.c - 1}, device_id_type=MESH)

    def up(self, b, t, d):
        block = self.c - t
        src = self.white.at[self.w, b] if t == 0 and d == 0 else self.rows.at[b, block, d]
        return pltpu.make_async_remote_copy(
            src_ref=src, dst_ref=self.rows.at[b, block, d],
            send_sem=self.up_send.at[b, t, d], recv_sem=self.up_recv.at[b, t, d],
            device_id={"col": self.c + 1}, device_id_type=MESH)

    def landed(self, b, block, d, sem):
        ref = self.rows.at[b, block, d]
        pltpu.make_async_copy(ref, ref, sem).wait()

    def col_keep(self, b, q):
        return pltpu.make_async_copy(
            self.rows.at[b, self.first_col + q], self.cols.at[b, q], self.col_own.at[b, q])

    def col_pass(self, b, q, e):
        return pltpu.make_async_remote_copy(
            src_ref=self.rows.at[b, self.first_col + q], dst_ref=self.cols.at[b, q],
            send_sem=self.col_send.at[b, q, e], recv_sem=self.col_recv.at[b, q],
            device_id={"row": (self.r + e) % self.R}, device_id_type=MESH)

    def start_swaps(self, b):
        self.keep(b).start()
        for d in range(1, self.S):
            self.swap(b, d).start()

    def down_goes(self, t):
        return jnp.logical_and(self.c > 0, self.c + t < self.N)

    def up_goes(self, t):
        return jnp.logical_and(self.c < self.N - 1, self.c - t >= 0)

    def send_own(self, b):
        for d in range(self.S):
            if d:
                self.landed(b, self.c, d, self.swap_recv.at[b, d])
            pl.when(self.down_goes(0))(lambda d=d: self.down(b, 0, d).start())
            pl.when(self.up_goes(0))(lambda d=d: self.up(b, 0, d).start())

    def forward_slot(self, b, t, d):
        @pl.when(self.c + t < self.N)
        def _():
            self.landed(b, self.c + t, d, self.down_recv.at[b, t - 1, d])

        if t < self.N - 1:
            pl.when(self.down_goes(t))(lambda: self.down(b, t, d).start())

        @pl.when(self.c - t >= 0)
        def _():
            self.landed(b, self.c - t, d, self.up_recv.at[b, t - 1, d])

        if t < self.N - 1:
            pl.when(self.up_goes(t))(lambda: self.up(b, t, d).start())

        if t == self.col_reach and d == self.S - 1:
            self.start_cols(b)

    def start_cols(self, b):
        self.keep(b).wait()

        @pl.when(self.is_root)
        def _():
            for q in range(self.R):
                for e in range(1, self.R):
                    self.col_pass(b, q, e).start()
                self.col_keep(b, q).start()

    def wait_cols(self, b):
        for q in range(self.R):
            @pl.when(self.is_root)
            def _():
                self.col_keep(b, q).wait()

            @pl.when(jnp.logical_not(self.is_root))
            def _():
                ref = self.cols.at[b, q]
                pltpu.make_async_copy(ref, ref, self.col_recv.at[b, q]).wait()

    def wait_sends(self):
        for b in range(self.bins):
            for d in range(1, self.S):
                self.swap(b, d).wait_send()
            for t in range(self.N - 1):
                for d in range(self.S):
                    pl.when(self.down_goes(t))(lambda: self.down(b, t, d).wait_send())
                    pl.when(self.up_goes(t))(lambda: self.up(b, t, d).wait_send())

            @pl.when(self.is_root)
            def _():
                for q in range(self.R):
                    for e in range(1, self.R):
                        self.col_pass(b, q, e).wait_send()


def gather_kernel(sizes, white, rows, cols, *sems):
    g = Gather(sizes, white, rows, cols, sems)
    g.barrier()
    g.start_swaps(0)
    g.send_own(0)
    for b in range(g.bins):
        if b + 1 < g.bins:
            g.start_swaps(b + 1)
        for t in range(1, g.N):
            for d in range(g.S):
                g.forward_slot(b, t, d)
            if t == 1 and b + 1 < g.bins:
                g.send_own(b + 1)
    for b in range(g.bins):
        g.wait_cols(b)
    g.wait_sends()


def gather_semaphores(sizes, bins):
    S, R, N = sizes
    dma = pltpu.SemaphoreType.DMA
    return [
        dma((bins,)), dma((bins, S)), dma((bins, S)),
        dma((bins, N, S)), dma((bins, N, S)), dma((bins, N, S)), dma((bins, N, S)),
        dma((bins, R)), dma((bins, R, R)), dma((bins, R)),
    ]


def gather(white, sizes):
    S, R, N = sizes
    _, bins, parts, windows, channels = white.shape
    slot = (parts, windows, channels)
    return pl.pallas_call(
        functools.partial(gather_kernel, sizes),
        out_shape=(
            jax.ShapeDtypeStruct((bins, N, S) + slot, white.dtype),
            jax.ShapeDtypeStruct((bins, R, S) + slot, white.dtype),
        ),
        in_specs=[pl.BlockSpec(memory_space=pl.ANY)],
        out_specs=(pl.BlockSpec(memory_space=pl.ANY), pl.BlockSpec(memory_space=pl.ANY)),
        scratch_shapes=gather_semaphores(sizes, bins),
        compiler_params=pltpu.CompilerParams(collective_id=0, has_side_effects=True),
    )(white)


def turn(right, S):
    depth = right.shape[0] // (2 * S)
    pieces = []
    for s in range(S):
        base = 2 * s * depth
        pieces.append(-right[base + depth:base + 2 * depth])
        pieces.append(right[base:base + depth])
    return jnp.concatenate(pieces, axis=0)


def stack_kernel(S, windows, left_ref, right_ref, out_ref, turned_ref):
    blocks, _, width = right_ref.shape[1:]

    @pl.when(pl.program_id(1) == 0)
    def _():
        for q in range(blocks):
            turned_ref[q] = turn(right_ref[0, q], S)

    left = left_ref[0, 0].T
    for q in range(blocks):
        where = slice(q * width, (q + 1) * width)
        real = jnp.dot(left, right_ref[0, q], preferred_element_type=jnp.float32)
        out_ref[0, 0, :, where] = real * (1.0 / windows)
        imag = jnp.dot(left, turned_ref[q], preferred_element_type=jnp.float32)
        out_ref[1, 0, :, where] = imag * (1.0 / windows)


def stack(rows, cols, S):
    bins, N, depth, channels = rows.shape
    R = cols.shape[1]
    tile = 384 if channels % 384 == 0 else 128
    per = channels // tile
    flops = 2 * 2 * bins * N * channels * R * channels * depth
    return pl.pallas_call(
        functools.partial(stack_kernel, S, depth // 2),
        grid=(bins, N * per),
        out_shape=jax.ShapeDtypeStruct((2, bins, N * channels, R * channels), jnp.float32),
        in_specs=[
            pl.BlockSpec((1, 1, depth, tile), lambda f, i: (f, i // per, 0, i % per)),
            pl.BlockSpec((1, R, depth, channels), lambda f, i: (f, 0, 0, 0)),
        ],
        out_specs=pl.BlockSpec((2, 1, tile, R * channels), lambda f, i: (0, f, i, 0)),
        scratch_shapes=[pltpu.VMEM((R, depth, channels), jnp.bfloat16)],
        compiler_params=pltpu.CompilerParams(vmem_limit_bytes=56 * 2**20),
        cost_estimate=pl.CostEstimate(flops=flops, bytes_accessed=10**8, transcendentals=0),
    )(rows, cols)


def per_device(sizes, spectra, gain):
    S, R, N = sizes
    parts, bins, channels, windows = spectra.shape
    white = whiten(spectra, gain)
    white = white.reshape(S, bins // S, parts, windows, channels)
    rows, cols = gather(white, sizes)
    depth = S * parts * windows
    rows = rows.reshape(bins // S, N, depth, channels)
    cols = cols.reshape(bins // S, R, depth, channels)
    return stack(rows, cols, S)


def solution(mesh):
    sizes = mesh.shape["win"], mesh.shape["row"], mesh.shape["col"]
    in_specs = (P(None, None, ("row", "col"), "win"), P(("row", "col")))
    out_specs = P(None, "win", "row", "col")

    def device_program(spectra, gain):
        S, R, N = sizes
        _, bins, channels, windows = spectra.shape
        whole_tiles = channels % 128 == 0 and windows % 16 == 0
        if whole_tiles and S % 2 == 0 and bins % S == 0 and N % R == 0 and R > 1:
            return per_device(sizes, spectra, gain)
        return per_device_collectives(spectra, gain)

    return jax.shard_map(
        device_program, mesh=mesh, in_specs=in_specs, out_specs=out_specs, check_vma=False
    )
```

```python
import functools

import jax
import jax.numpy as jnp
from jax import lax
from jax.experimental import pallas as pl
from jax.experimental.pallas import tpu as pltpu
from jax.sharding import PartitionSpec as P

MESH = pl.DeviceIdType.MESH


def broadcast(value, axis, source):
    kept = jnp.where(lax.axis_index(axis) == source, value, 0).astype(value.dtype)
    return lax.psum(kept, axis)


def per_device_collectives(spectra, gain):
    calibrated = spectra.astype(jnp.float32) * gain[None, None, :, None]
    level = jnp.sqrt(jnp.mean(calibrated * calibrated, axis=(0, 1)))
    white = (calibrated / jnp.maximum(level, 0.5)).astype(jnp.bfloat16)
    regrouped = lax.all_to_all(white, "win", split_axis=1, concat_axis=3, tiled=True)
    windows = regrouped.shape[3]
    rows_block = lax.all_gather(regrouped, "col", axis=2, tiled=True)
    ratio = lax.axis_size("col") // lax.axis_size("row")
    col_width = rows_block.shape[2] // ratio
    col_index = lax.axis_index("col")
    portion = col_index % ratio
    root_row = col_index // ratio
    relayed = broadcast(rows_block, "row", root_row)
    cols_block = lax.dynamic_slice_in_dim(relayed, portion * col_width, col_width, 2)
    left_side = jnp.concatenate([rows_block[0], rows_block[1]], axis=-1)
    right_real = jnp.concatenate([cols_block[0], cols_block[1]], axis=-1)
    right_imag = jnp.concatenate([-cols_block[1], cols_block[0]], axis=-1)
    right_both = jnp.stack([right_real, right_imag])
    stacked = jnp.einsum(
        "fiw,ofjw->ofij", left_side, right_both, preferred_element_type=jnp.float32
    )
    return stacked / jnp.float32(windows)


def whiten_kernel(x_ref, gain_ref, white_ref):
    parts, bins = x_ref.shape[:2]
    gain = gain_ref[...]
    total = jnp.zeros(x_ref.shape[2:], jnp.float32)
    for p in range(parts):
        for f in range(bins):
            calibrated = x_ref[p, f].astype(jnp.float32) * gain
            total += calibrated * calibrated
    level = jnp.sqrt(total * (1.0 / (parts * bins)))
    scale = 1.0 / jnp.maximum(level, 0.5)
    for p in range(parts):
        for f in range(bins):
            calibrated = x_ref[p, f].astype(jnp.float32) * gain
            white_ref[f, p] = (calibrated * scale).astype(white_ref.dtype)


def whiten(spectra, gain):
    parts, bins, channels, windows = spectra.shape
    tile = 32 if windows % 32 == 0 else 16
    return pl.pallas_call(
        whiten_kernel,
        grid=(windows // tile,),
        out_shape=jax.ShapeDtypeStruct((bins, parts, windows, channels), jnp.bfloat16),
        in_specs=[
            pl.BlockSpec((parts, bins, tile, channels), lambda i: (0, 0, i, 0)),
            pl.BlockSpec((1, channels), lambda i: (0, 0)),
        ],
        out_specs=pl.BlockSpec((bins, parts, tile, channels), lambda i: (0, 0, i, 0)),
        compiler_params=pltpu.CompilerParams(vmem_limit_bytes=32 * 2**20),
    )(jnp.swapaxes(spectra, 2, 3), gain[None])


class Gather:
    def __init__(self, sizes, white, rows, cols, sems):
        self.S, self.R, self.N = sizes
        self.white, self.rows, self.cols = white, rows, cols
        (self.own_sem, self.swap_send, self.swap_recv, self.down_send, self.down_recv, self.up_send, self.up_recv,
         self.col_send, self.col_recv, self.right_sem) = sems
        self.w, self.r, self.c = lax.axis_index("win"), lax.axis_index("row"), lax.axis_index("col")
        self.bins = rows.shape[0]
        ratio = self.N // self.R
        self.first_col = (self.c % ratio) * self.R
        self.is_root = self.r == self.c // ratio
        self.col_reach = max(
            abs((c % ratio) * self.R + q - c) for c in range(self.N) for q in range(self.R)
        )

    def partner(self, d):
        half = self.S // 2
        return ((self.w // 2 + d // 2) % half) * 2 + (self.w + d) % 2

    def barrier(self):
        sem = pltpu.get_barrier_semaphore()
        for d in range(1, self.S):
            pl.semaphore_signal(sem, inc=1, device_id={"win": self.partner(d)}, device_id_type=MESH)
        for e in range(1, self.R):
            pl.semaphore_signal(sem, inc=1, device_id={"row": (self.r + e) % self.R}, device_id_type=MESH)

        @pl.when(self.c > 0)
        def _():
            pl.semaphore_signal(sem, inc=1, device_id={"col": self.c - 1}, device_id_type=MESH)

        @pl.when(self.c < self.N - 1)
        def _():
            pl.semaphore_signal(sem, inc=1, device_id={"col": self.c + 1}, device_id_type=MESH)

        ends = (self.c == 0).astype(jnp.int32) + (self.c == self.N - 1).astype(jnp.int32)
        pl.semaphore_wait(sem, self.S - 1 + self.R - 1 + 2 - ends)

    def keep(self, b):
        return pltpu.make_async_copy(self.white.at[self.w, b], self.rows.at[b, self.c, 0], self.own_sem.at[b])

    def swap(self, b, d):
        p = self.partner(d)
        return pltpu.make_async_remote_copy(
            src_ref=self.white.at[p, b], dst_ref=self.rows.at[b, self.c, d],
            send_sem=self.swap_send.at[b, d], recv_sem=self.swap_recv.at[b, d],
            device_id={"win": p}, device_id_type=MESH)

    def down(self, b, t, d):
        block = self.c + t
        src = self.white.at[self.w, b] if t == 0 and d == 0 else self.rows.at[b, block, d]
        return pltpu.make_async_remote_copy(
            src_ref=src, dst_ref=self.rows.at[b, block, d],
            send_sem=self.down_send.at[b, t, d], recv_sem=self.down_recv.at[b, t, d],
            device_id={"col": self.c - 1}, device_id_type=MESH)

    def up(self, b, t, d):
        block = self.c - t
        src = self.white.at[self.w, b] if t == 0 and d == 0 else self.rows.at[b, block, d]
        return pltpu.make_async_remote_copy(
            src_ref=src, dst_ref=self.rows.at[b, block, d],
            send_sem=self.up_send.at[b, t, d], recv_sem=self.up_recv.at[b, t, d],
            device_id={"col": self.c + 1}, device_id_type=MESH)

    def landed(self, b, block, d, sem):
        ref = self.rows.at[b, block, d]
        pltpu.make_async_copy(ref, ref, sem).wait()

    def col_pass(self, b, q, e):
        return pltpu.make_async_remote_copy(
            src_ref=self.rows.at[b, self.first_col + q], dst_ref=self.cols.at[b, q],
            send_sem=self.col_send.at[b, q, e], recv_sem=self.col_recv.at[b, q],
            device_id={"row": (self.r + e) % self.R}, device_id_type=MESH)

    def start_swaps(self, b):
        self.keep(b).start()
        for d in range(1, self.S):
            self.swap(b, d).start()

    def down_goes(self, t):
        return jnp.logical_and(self.c > 0, self.c + t < self.N)

    def up_goes(self, t):
        return jnp.logical_and(self.c < self.N - 1, self.c - t >= 0)

    def send_own(self, b):
        for d in range(self.S):
            if d:
                self.landed(b, self.c, d, self.swap_recv.at[b, d])
            pl.when(self.down_goes(0))(lambda d=d: self.down(b, 0, d).start())
            pl.when(self.up_goes(0))(lambda d=d: self.up(b, 0, d).start())

    def forward_slot(self, b, t, d):
        @pl.when(self.c + t < self.N)
        def _():
            self.landed(b, self.c + t, d, self.down_recv.at[b, t - 1, d])

        if t < self.N - 1:
            pl.when(self.down_goes(t))(lambda: self.down(b, t, d).start())

        @pl.when(self.c - t >= 0)
        def _():
            self.landed(b, self.c - t, d, self.up_recv.at[b, t - 1, d])

        if t < self.N - 1:
            pl.when(self.up_goes(t))(lambda: self.up(b, t, d).start())

        if t == self.col_reach and d == self.S - 1:
            self.start_cols(b)

    def start_cols(self, b):
        self.keep(b).wait()

        @pl.when(self.is_root)
        def _():
            for q in range(self.R):
                for e in range(1, self.R):
                    self.col_pass(b, q, e).start()

    def wait_cols(self, b):
        @pl.when(jnp.logical_not(self.is_root))
        def _():
            for q in range(self.R):
                ref = self.cols.at[b, q]
                pltpu.make_async_copy(ref, ref, self.col_recv.at[b, q]).wait()

    def wait_sends(self):
        for b in range(self.bins):
            for d in range(1, self.S):
                self.swap(b, d).wait_send()
            for t in range(self.N - 1):
                for d in range(self.S):
                    pl.when(self.down_goes(t))(lambda: self.down(b, t, d).wait_send())
                    pl.when(self.up_goes(t))(lambda: self.up(b, t, d).wait_send())

            @pl.when(self.is_root)
            def _():
                for q in range(self.R):
                    for e in range(1, self.R):
                        self.col_pass(b, q, e).wait_send()


def load_right(rows, cols, b, right, turned, sem):
    R, S, depth, _ = right.shape
    half = depth // 2
    row, col = lax.axis_index("row"), lax.axis_index("col")
    ratio = rows.shape[1] // R
    first, is_root = (col % ratio) * R, row == col // ratio

    @pl.when(is_root)
    def _():
        for q in range(R):
            pltpu.make_async_copy(rows.at[b, first + q], right.at[q], sem.at[q]).start()

    @pl.when(jnp.logical_not(is_root))
    def _():
        for q in range(R):
            pltpu.make_async_copy(cols.at[b, q], right.at[q], sem.at[q]).start()

    for q in range(R):
        pltpu.make_async_copy(cols.at[b, q], right.at[q], sem.at[q]).wait()
        for s in range(S):
            turned[q, s, :half] = -right[q, s, half:]
            turned[q, s, half:] = right[q, s, :half]


def stack_tile(left, right, turned, put):
    R, S, depth, width = right.shape
    scale = 2.0 / (S * depth)
    left = left.reshape(S * depth, left.shape[-1]).T
    for q in range(R):
        for part, side in enumerate((right, turned)):
            block = side[q].reshape(S * depth, width)
            total = jnp.dot(left, block, preferred_element_type=jnp.float32)
            put(part, slice(q * width, (q + 1) * width), total * scale)


def tile_of(channels):
    return 384 if channels % 384 == 0 else 128


def stack_early(g, b, early, left_buf, right, turned, out_buf, left_sem, out_sem):
    load_right(g.rows, g.cols, b, right, turned, g.right_sem)
    channels = right.shape[-1]
    tile = left_buf.shape[-1]
    per = channels // tile
    count = g.N * per

    def fetch(i):
        lanes = pl.ds(pl.multiple_of((i % per) * tile, 128), tile)
        return pltpu.make_async_copy(
            g.rows.at[b, i // per, :, :, lanes], left_buf.at[i % 2], left_sem.at[i % 2])

    def flush(i):
        return pltpu.make_async_copy(
            out_buf.at[i % 2], early.at[:, pl.ds(pl.multiple_of(i * tile, 128), tile), :], out_sem.at[i % 2])

    fetch(0).start()

    def step(i, carry):
        pl.when(i + 1 < count)(lambda: fetch(i + 1).start())
        fetch(i).wait()
        pl.when(i >= 2)(lambda: flush(i - 2).wait())

        def put(part, lanes, value):
            out_buf[i % 2, part, :, lanes] = value

        stack_tile(left_buf[i % 2], right, turned, put)
        flush(i).start()
        return carry

    lax.fori_loop(0, count, step, 0)
    flush(count - 2).wait()
    flush(count - 1).wait()


def gather_kernel(sizes, white, rows, cols, early, left_buf, right, turned, out_buf, left_sem, out_sem, *sems):
    g = Gather(sizes, white, rows, cols, sems)
    g.barrier()
    g.start_swaps(0)
    g.send_own(0)
    for b in range(g.bins):
        if b + 1 < g.bins:
            g.start_swaps(b + 1)
        for t in range(1, g.N):
            for d in range(g.S):
                g.forward_slot(b, t, d)
            if t == 1 and b + 1 < g.bins:
                g.send_own(b + 1)
        g.wait_cols(b)
        if b == 0:
            stack_early(g, b, early, left_buf, right, turned, out_buf, left_sem, out_sem)
    g.wait_sends()


def gather_semaphores(sizes, bins):
    S, R, N = sizes
    dma = pltpu.SemaphoreType.DMA
    return [
        dma((bins,)), dma((bins, S)), dma((bins, S)),
        dma((bins, N, S)), dma((bins, N, S)), dma((bins, N, S)), dma((bins, N, S)),
        dma((bins, R, R)), dma((bins, R)), dma((R,)),
    ]


def gather(white, sizes):
    S, R, N = sizes
    _, bins, depth, channels = white.shape
    tile = tile_of(channels)
    flops = 2 * 2 * N * channels * R * channels * S * depth
    return pl.pallas_call(
        functools.partial(gather_kernel, sizes),
        out_shape=(
            jax.ShapeDtypeStruct((bins, N, S, depth, channels), white.dtype),
            jax.ShapeDtypeStruct((bins, R, S, depth, channels), white.dtype),
            jax.ShapeDtypeStruct((2, N * channels, R * channels), jnp.float32),
        ),
        in_specs=[pl.BlockSpec(memory_space=pl.ANY)],
        out_specs=(pl.BlockSpec(memory_space=pl.ANY),) * 3,
        scratch_shapes=[
            pltpu.VMEM((2, S, depth, tile), white.dtype),
            pltpu.VMEM((R, S, depth, channels), white.dtype),
            pltpu.VMEM((R, S, depth, channels), white.dtype),
            pltpu.VMEM((2, 2, tile, R * channels), jnp.float32),
            pltpu.SemaphoreType.DMA((2,)),
            pltpu.SemaphoreType.DMA((2,)),
        ] + gather_semaphores(sizes, bins),
        compiler_params=pltpu.CompilerParams(
            collective_id=0, has_side_effects=True, vmem_limit_bytes=48 * 2**20),
        cost_estimate=pl.CostEstimate(flops=flops, bytes_accessed=10**8, transcendentals=0),
    )(white)


def stack_kernel(left_ref, early_ref, rows, cols, out_ref, right, turned, sem):
    @pl.when(pl.program_id(0) == 0)
    def _():
        load_right(rows, cols, 1, right, turned, sem)

    out_ref[:, 0] = early_ref[...]

    def put(part, lanes, value):
        out_ref[part, 1, :, lanes] = value

    stack_tile(left_ref[0, 0], right, turned, put)


def stack(rows, cols, early):
    bins, N, S, depth, channels = rows.shape
    R = cols.shape[1]
    tile = tile_of(channels)
    per = channels // tile
    flops = 2 * 2 * N * channels * R * channels * S * depth
    return pl.pallas_call(
        stack_kernel,
        grid=(N * per,),
        out_shape=jax.ShapeDtypeStruct((2, bins, N * channels, R * channels), jnp.float32),
        in_specs=[
            pl.BlockSpec((1, 1, S, depth, tile), lambda i: (1, i // per, 0, 0, i % per)),
            pl.BlockSpec((2, tile, R * channels), lambda i: (0, i, 0)),
            pl.BlockSpec(memory_space=pl.ANY),
            pl.BlockSpec(memory_space=pl.ANY),
        ],
        out_specs=pl.BlockSpec((2, bins, tile, R * channels), lambda i: (0, 0, i, 0)),
        scratch_shapes=[
            pltpu.VMEM((R, S, depth, channels), rows.dtype),
            pltpu.VMEM((R, S, depth, channels), rows.dtype),
            pltpu.SemaphoreType.DMA((R,)),
        ],
        compiler_params=pltpu.CompilerParams(vmem_limit_bytes=56 * 2**20),
        cost_estimate=pl.CostEstimate(flops=flops, bytes_accessed=12 * 10**7, transcendentals=0),
    )(rows, early, rows, cols)


def per_device(sizes, spectra, gain):
    S, R, N = sizes
    parts, bins, channels, windows = spectra.shape
    white = whiten(spectra, gain).reshape(S, bins // S, parts * windows, channels)
    rows, cols, early = gather(white, sizes)
    return stack(rows, cols, early)


def solution(mesh):
    sizes = mesh.shape["win"], mesh.shape["row"], mesh.shape["col"]
    in_specs = (P(None, None, ("row", "col"), "win"), P(("row", "col")))
    out_specs = P(None, "win", "row", "col")

    def device_program(spectra, gain):
        S, R, N = sizes
        _, bins, channels, windows = spectra.shape
        whole_tiles = channels % 128 == 0 and windows % 16 == 0
        if whole_tiles and S % 2 == 0 and bins == 2 * S and N % R == 0 and R > 1:
            return per_device(sizes, spectra, gain)
        return per_device_collectives(spectra, gain)

    return jax.shard_map(
        device_program, mesh=mesh, in_specs=in_specs, out_specs=out_specs, check_vma=False
    )
```

```python
import functools

import jax
import jax.numpy as jnp
from jax import lax
from jax.experimental import pallas as pl
from jax.experimental.pallas import tpu as pltpu
from jax.sharding import PartitionSpec as P

MESH = pl.DeviceIdType.MESH


def broadcast(value, axis, source):
    kept = jnp.where(lax.axis_index(axis) == source, value, 0).astype(value.dtype)
    return lax.psum(kept, axis)


def per_device_collectives(spectra, gain):
    calibrated = spectra.astype(jnp.float32) * gain[None, None, :, None]
    level = jnp.sqrt(jnp.mean(calibrated * calibrated, axis=(0, 1)))
    white = (calibrated / jnp.maximum(level, 0.5)).astype(jnp.bfloat16)
    regrouped = lax.all_to_all(white, "win", split_axis=1, concat_axis=3, tiled=True)
    windows = regrouped.shape[3]
    rows_block = lax.all_gather(regrouped, "col", axis=2, tiled=True)
    ratio = lax.axis_size("col") // lax.axis_size("row")
    col_width = rows_block.shape[2] // ratio
    col_index = lax.axis_index("col")
    portion = col_index % ratio
    root_row = col_index // ratio
    relayed = broadcast(rows_block, "row", root_row)
    cols_block = lax.dynamic_slice_in_dim(relayed, portion * col_width, col_width, 2)
    left_side = jnp.concatenate([rows_block[0], rows_block[1]], axis=-1)
    right_real = jnp.concatenate([cols_block[0], cols_block[1]], axis=-1)
    right_imag = jnp.concatenate([-cols_block[1], cols_block[0]], axis=-1)
    right_both = jnp.stack([right_real, right_imag])
    stacked = jnp.einsum(
        "fiw,ofjw->ofij", left_side, right_both, preferred_element_type=jnp.float32
    )
    return stacked / jnp.float32(windows)


def whiten_kernel(x_ref, gain_ref, white_ref):
    parts, bins = x_ref.shape[:2]
    gain = gain_ref[...]
    total = jnp.zeros(x_ref.shape[2:], jnp.float32)
    for p in range(parts):
        for f in range(bins):
            calibrated = x_ref[p, f].astype(jnp.float32) * gain
            total += calibrated * calibrated
    level = jnp.sqrt(total * (1.0 / (parts * bins)))
    scale = 1.0 / jnp.maximum(level, 0.5)
    for p in range(parts):
        for f in range(bins):
            calibrated = x_ref[p, f].astype(jnp.float32) * gain
            white_ref[f, p] = (calibrated * scale).astype(white_ref.dtype)


def whiten(spectra, gain):
    parts, bins, channels, windows = spectra.shape
    tile = 32 if windows % 32 == 0 else 16
    return pl.pallas_call(
        whiten_kernel,
        grid=(windows // tile,),
        out_shape=jax.ShapeDtypeStruct((bins, parts, windows, channels), jnp.bfloat16),
        in_specs=[
            pl.BlockSpec((parts, bins, tile, channels), lambda i: (0, 0, i, 0)),
            pl.BlockSpec((1, channels), lambda i: (0, 0)),
        ],
        out_specs=pl.BlockSpec((bins, parts, tile, channels), lambda i: (0, 0, i, 0)),
        compiler_params=pltpu.CompilerParams(vmem_limit_bytes=32 * 2**20),
    )(jnp.swapaxes(spectra, 2, 3), gain[None])


class Gather:
    def __init__(self, sizes, white, rows, cols, sems):
        self.S, self.R, self.N = sizes
        self.white, self.rows, self.cols = white, rows, cols
        (self.own_sem, self.swap_send, self.swap_recv, self.down_send, self.down_recv, self.up_send, self.up_recv,
         self.col_send, self.col_recv, self.right_sem) = sems
        self.w, self.r, self.c = lax.axis_index("win"), lax.axis_index("row"), lax.axis_index("col")
        self.bins = rows.shape[0]
        ratio = self.N // self.R
        self.first_col = (self.c % ratio) * self.R
        self.is_root = self.r == self.c // ratio
        self.col_reach = max(
            abs((c % ratio) * self.R + q - c) for c in range(self.N) for q in range(self.R)
        )

    def partner(self, d):
        half = self.S // 2
        return ((self.w // 2 + d // 2) % half) * 2 + (self.w + d) % 2

    def barrier(self):
        sem = pltpu.get_barrier_semaphore()
        for d in range(1, self.S):
            pl.semaphore_signal(sem, inc=1, device_id={"win": self.partner(d)}, device_id_type=MESH)
        for e in range(1, self.R):
            pl.semaphore_signal(sem, inc=1, device_id={"row": (self.r + e) % self.R}, device_id_type=MESH)

        @pl.when(self.c > 0)
        def _():
            pl.semaphore_signal(sem, inc=1, device_id={"col": self.c - 1}, device_id_type=MESH)

        @pl.when(self.c < self.N - 1)
        def _():
            pl.semaphore_signal(sem, inc=1, device_id={"col": self.c + 1}, device_id_type=MESH)

        ends = (self.c == 0).astype(jnp.int32) + (self.c == self.N - 1).astype(jnp.int32)
        pl.semaphore_wait(sem, self.S - 1 + self.R - 1 + 2 - ends)

    def keep(self, b):
        return pltpu.make_async_copy(self.white.at[self.w, b], self.rows.at[b, self.c, 0], self.own_sem.at[b])

    def swap(self, b, d):
        p = self.partner(d)
        return pltpu.make_async_remote_copy(
            src_ref=self.white.at[p, b], dst_ref=self.rows.at[b, self.c, d],
            send_sem=self.swap_send.at[b, d], recv_sem=self.swap_recv.at[b, d],
            device_id={"win": p}, device_id_type=MESH)

    def down(self, b, t, d):
        block = self.c + t
        src = self.white.at[self.w, b] if t == 0 and d == 0 else self.rows.at[b, block, d]
        return pltpu.make_async_remote_copy(
            src_ref=src, dst_ref=self.rows.at[b, block, d],
            send_sem=self.down_send.at[b, t, d], recv_sem=self.down_recv.at[b, t, d],
            device_id={"col": self.c - 1}, device_id_type=MESH)

    def up(self, b, t, d):
        block = self.c - t
        src = self.white.at[self.w, b] if t == 0 and d == 0 else self.rows.at[b, block, d]
        return pltpu.make_async_remote_copy(
            src_ref=src, dst_ref=self.rows.at[b, block, d],
            send_sem=self.up_send.at[b, t, d], recv_sem=self.up_recv.at[b, t, d],
            device_id={"col": self.c + 1}, device_id_type=MESH)

    def landed(self, b, block, d, sem):
        ref = self.rows.at[b, block, d]
        pltpu.make_async_copy(ref, ref, sem).wait()

    def col_pass(self, b, q, e):
        return pltpu.make_async_remote_copy(
            src_ref=self.rows.at[b, self.first_col + q], dst_ref=self.cols.at[b, q],
            send_sem=self.col_send.at[b, q, e], recv_sem=self.col_recv.at[b, q],
            device_id={"row": (self.r + e) % self.R}, device_id_type=MESH)

    def start_swaps(self, b):
        self.keep(b).start()
        for d in range(1, self.S):
            self.swap(b, d).start()

    def down_goes(self, t):
        return jnp.logical_and(self.c > 0, self.c + t < self.N)

    def up_goes(self, t):
        return jnp.logical_and(self.c < self.N - 1, self.c - t >= 0)

    def send_own(self, b):
        for d in range(self.S):
            if d:
                self.landed(b, self.c, d, self.swap_recv.at[b, d])
            pl.when(self.down_goes(0))(lambda d=d: self.down(b, 0, d).start())
            pl.when(self.up_goes(0))(lambda d=d: self.up(b, 0, d).start())

    def forward_slot(self, b, t, d):
        @pl.when(self.c + t < self.N)
        def _():
            self.landed(b, self.c + t, d, self.down_recv.at[b, t - 1, d])

        if t < self.N - 1:
            pl.when(self.down_goes(t))(lambda: self.down(b, t, d).start())

        @pl.when(self.c - t >= 0)
        def _():
            self.landed(b, self.c - t, d, self.up_recv.at[b, t - 1, d])

        if t < self.N - 1:
            pl.when(self.up_goes(t))(lambda: self.up(b, t, d).start())

        if t == self.col_reach and d == self.S - 1:
            self.start_cols(b)

    def start_cols(self, b):
        self.keep(b).wait()

        @pl.when(self.is_root)
        def _():
            for q in range(self.R):
                for e in range(1, self.R):
                    self.col_pass(b, q, e).start()

    def wait_cols(self, b):
        @pl.when(jnp.logical_not(self.is_root))
        def _():
            for q in range(self.R):
                ref = self.cols.at[b, q]
                pltpu.make_async_copy(ref, ref, self.col_recv.at[b, q]).wait()

    def wait_sends(self):
        for b in range(self.bins):
            for d in range(1, self.S):
                self.swap(b, d).wait_send()
            for t in range(self.N - 1):
                for d in range(self.S):
                    pl.when(self.down_goes(t))(lambda: self.down(b, t, d).wait_send())
                    pl.when(self.up_goes(t))(lambda: self.up(b, t, d).wait_send())

            @pl.when(self.is_root)
            def _():
                for q in range(self.R):
                    for e in range(1, self.R):
                        self.col_pass(b, q, e).wait_send()


def load_right(rows, cols, b, right, turned, sem, meanwhile=None):
    R, S, depth, _ = right.shape
    half = depth // 2
    row, col = lax.axis_index("row"), lax.axis_index("col")
    ratio = rows.shape[1] // R
    first, is_root = (col % ratio) * R, row == col // ratio

    @pl.when(is_root)
    def _():
        for q in range(R):
            pltpu.make_async_copy(rows.at[b, first + q], right.at[q], sem.at[q]).start()

    @pl.when(jnp.logical_not(is_root))
    def _():
        for q in range(R):
            pltpu.make_async_copy(cols.at[b, q], right.at[q], sem.at[q]).start()

    if meanwhile is not None:
        meanwhile()
    for q in range(R):
        pltpu.make_async_copy(cols.at[b, q], right.at[q], sem.at[q]).wait()
        for s in range(S):
            turned[q, s, :half] = -right[q, s, half:]
            turned[q, s, half:] = right[q, s, :half]


def stack_tile(left, right, turned, put):
    R, S, depth, width = right.shape
    scale = 2.0 / (S * depth)
    left = left.reshape(S * depth, left.shape[-1]).T
    for q in range(R):
        for part, side in enumerate((right, turned)):
            block = side[q].reshape(S * depth, width)
            total = jnp.dot(left, block, preferred_element_type=jnp.float32)
            put(part, slice(q * width, (q + 1) * width), total * scale)


def tile_of(channels):
    return 384 if channels % 384 == 0 else 128


def stack_early(g, b, early, left_buf, right, turned, out_buf, left_sem, out_sem):
    load_right(g.rows, g.cols, b, right, turned, g.right_sem)
    channels = right.shape[-1]
    tile = left_buf.shape[-1]
    per = channels // tile
    count = g.N * per

    def fetch(i):
        lanes = pl.ds(pl.multiple_of((i % per) * tile, 128), tile)
        return pltpu.make_async_copy(
            g.rows.at[b, i // per, :, :, lanes], left_buf.at[i % 2], left_sem.at[i % 2])

    def flush(i):
        return pltpu.make_async_copy(
            out_buf.at[i % 2], early.at[:, pl.ds(pl.multiple_of(i * tile, 128), tile), :], out_sem.at[i % 2])

    fetch(0).start()

    def step(i, carry):
        pl.when(i + 1 < count)(lambda: fetch(i + 1).start())
        fetch(i).wait()
        pl.when(i >= 2)(lambda: flush(i - 2).wait())

        def put(part, lanes, value):
            out_buf[i % 2, part, :, lanes] = value.astype(out_buf.dtype)

        stack_tile(left_buf[i % 2], right, turned, put)
        flush(i).start()
        return carry

    lax.fori_loop(0, count, step, 0)
    flush(count - 2).wait()
    flush(count - 1).wait()


def gather_kernel(sizes, white, rows, cols, early, left_buf, right, turned, out_buf, left_sem, out_sem, *sems):
    g = Gather(sizes, white, rows, cols, sems)
    g.barrier()
    g.start_swaps(0)
    g.send_own(0)
    for b in range(g.bins):
        if b + 1 < g.bins:
            g.start_swaps(b + 1)
        for t in range(1, g.N):
            for d in range(g.S):
                g.forward_slot(b, t, d)
            if t == 1 and b + 1 < g.bins:
                g.send_own(b + 1)
        g.wait_cols(b)
        if b == 0:
            stack_early(g, b, early, left_buf, right, turned, out_buf, left_sem, out_sem)
    g.wait_sends()


def gather_semaphores(sizes, bins):
    S, R, N = sizes
    dma = pltpu.SemaphoreType.DMA
    return [
        dma((bins,)), dma((bins, S)), dma((bins, S)),
        dma((bins, N, S)), dma((bins, N, S)), dma((bins, N, S)), dma((bins, N, S)),
        dma((bins, R, R)), dma((bins, R)), dma((R,)),
    ]


def gather(white, sizes):
    S, R, N = sizes
    _, bins, depth, channels = white.shape
    tile = tile_of(channels)
    flops = 2 * 2 * N * channels * R * channels * S * depth
    return pl.pallas_call(
        functools.partial(gather_kernel, sizes),
        out_shape=(
            jax.ShapeDtypeStruct((bins, N, S, depth, channels), white.dtype),
            jax.ShapeDtypeStruct((bins, R, S, depth, channels), white.dtype),
            jax.ShapeDtypeStruct((2, N * channels, R * channels), white.dtype),
        ),
        in_specs=[pl.BlockSpec(memory_space=pl.ANY)],
        out_specs=(pl.BlockSpec(memory_space=pl.ANY),) * 3,
        scratch_shapes=[
            pltpu.VMEM((2, S, depth, tile), white.dtype),
            pltpu.VMEM((R, S, depth, channels), white.dtype),
            pltpu.VMEM((R, S, depth, channels), white.dtype),
            pltpu.VMEM((2, 2, tile, R * channels), white.dtype),
            pltpu.SemaphoreType.DMA((2,)),
            pltpu.SemaphoreType.DMA((2,)),
        ] + gather_semaphores(sizes, bins),
        compiler_params=pltpu.CompilerParams(
            collective_id=0, has_side_effects=True, vmem_limit_bytes=48 * 2**20),
        cost_estimate=pl.CostEstimate(flops=flops, bytes_accessed=10**8, transcendentals=0),
    )(white)


def stack_kernel(left_ref, early_ref, rows, cols, out_ref, right, turned, sem):
    def place():
        out_ref[:, 0] = early_ref[...].astype(jnp.float32)

    first = pl.program_id(0) == 0
    pl.when(first)(lambda: load_right(rows, cols, 1, right, turned, sem, place))
    pl.when(jnp.logical_not(first))(place)

    def put(part, lanes, value):
        out_ref[part, 1, :, lanes] = value

    stack_tile(left_ref[0, 0], right, turned, put)


def stack(rows, cols, early):
    bins, N, S, depth, channels = rows.shape
    R = cols.shape[1]
    tile = tile_of(channels)
    per = channels // tile
    flops = 2 * 2 * N * channels * R * channels * S * depth
    return pl.pallas_call(
        stack_kernel,
        grid=(N * per,),
        out_shape=jax.ShapeDtypeStruct((2, bins, N * channels, R * channels), jnp.float32),
        in_specs=[
            pl.BlockSpec((1, 1, S, depth, tile), lambda i: (1, i // per, 0, 0, i % per)),
            pl.BlockSpec((2, tile, R * channels), lambda i: (0, i, 0)),
            pl.BlockSpec(memory_space=pl.ANY),
            pl.BlockSpec(memory_space=pl.ANY),
        ],
        out_specs=pl.BlockSpec((2, bins, tile, R * channels), lambda i: (0, 0, i, 0)),
        scratch_shapes=[
            pltpu.VMEM((R, S, depth, channels), rows.dtype),
            pltpu.VMEM((R, S, depth, channels), rows.dtype),
            pltpu.SemaphoreType.DMA((R,)),
        ],
        compiler_params=pltpu.CompilerParams(vmem_limit_bytes=56 * 2**20),
        cost_estimate=pl.CostEstimate(flops=flops, bytes_accessed=12 * 10**7, transcendentals=0),
    )(rows, early, rows, cols)


def per_device(sizes, spectra, gain):
    S, R, N = sizes
    parts, bins, channels, windows = spectra.shape
    white = whiten(spectra, gain).reshape(S, bins // S, parts * windows, channels)
    rows, cols, early = gather(white, sizes)
    return stack(rows, cols, early)


def solution(mesh):
    sizes = mesh.shape["win"], mesh.shape["row"], mesh.shape["col"]
    in_specs = (P(None, None, ("row", "col"), "win"), P(("row", "col")))
    out_specs = P(None, "win", "row", "col")

    def device_program(spectra, gain):
        S, R, N = sizes
        _, bins, channels, windows = spectra.shape
        whole_tiles = channels % 128 == 0 and windows % 16 == 0
        if whole_tiles and S % 2 == 0 and bins == 2 * S and N % R == 0 and R > 1:
            return per_device(sizes, spectra, gain)
        return per_device_collectives(spectra, gain)

    return jax.shard_map(
        device_program, mesh=mesh, in_specs=in_specs, out_specs=out_specs, check_vma=False
    )
```
